512 devices in a mesh: space: 32 (over x, y, core), mode: 16 (over z).
Axes of the slice: x: 4, y: 4, z: 16, core: 2. Of those that a mesh axis runs over, the one named last changes fastest.
Arguments:
- basis: bfloat16 [32, 5, 65536], P('mode', None, 'space'), may hold values from -144 to 144
- jacobian: bfloat16 [3, 5, 5, 65536], P(None, None, None, 'space'), may hold values from -1.5 to 1.5
- sample_list: int32 [32, 64], P('space'), may hold values from 0 to 511, as said below
- sample_weight: float32 [32, 64], P('space'), may hold values from 0.25 to 2
Outputs:
- update: float32 [32, 5, 65536], P('mode', None, 'space')
The draws below stay inside these ranges and needn't reach their ends.
Inputs may be any that keep to these rules, and one draw needn't show every extreme that they name: `sample_list`: row o holds 64 different tile numbers: exactly 4 from each of 16 different devices (device s holds tiles 16 * s to 16 * s + 15), one of which is device o itself, whose first and last tiles are in the row.
All inputs are finite; a program needn't handle non-finite values.
Results may differ from the reference program's by a relative error of at most 0.005.
Values may be sent and summed in bfloat16 or wider, within the bound.
A program may use at most 64 MiB of HBM per device.

```python
import math
import jax
import jax.numpy as jnp
from jax import lax

F = 5
PANEL = 32
TILE = 128
TILES_DEV = 16
CAP = 4
LIST = 64
TILES = 512
CELLS = 65536
N_SPACE = 32


def draw_basis(key, part):
    value_key = jax.random.fold_in(key, 0)
    jitter_key = jax.random.fold_in(key, 1)
    field_key = jax.random.fold_in(key, 3)
    mode_index = jnp.arange(PANEL, dtype=jnp.float32)
    jitter = jax.random.uniform(jitter_key, (PANEL,), jnp.float32, 0.8, 1.25)
    mode_scale = 0.3 * jnp.power(10.0, mode_index / max(PANEL - 1, 1)) * jitter
    field_scale = jnp.exp(jax.random.uniform(field_key, (F,), jnp.float32, 0.0, 1.1))
    values_raw = jax.random.truncated_normal(value_key, -4.0, 4.0, (PANEL, F, CELLS), jnp.float32)
    cell_index = jnp.arange(CELLS, dtype=jnp.int32)
    block_start = cell_index % (TILES_DEV * TILE) == 0
    cell_boost = jnp.where(block_start, 6.0, 1.0).astype(jnp.float32)
    return (values_raw * mode_scale[:, None, None] * field_scale[None, :, None] * 0.5 * cell_boost[None, None, :]).astype(jnp.bfloat16)


def draw_sample_list(key, part):
    space_count = TILES // TILES_DEV
    groups = LIST // CAP
    hot_key, owner_key = jax.random.split(key, 2)
    hot_order = jax.random.permutation(hot_key, space_count)
    hot = (hot_order < max(space_count // 4, 1)).astype(jnp.int32)
    devices = jnp.arange(space_count, dtype=jnp.int32)

    def one_owner(owner_index):
        owner_seed = jax.random.fold_in(owner_key, owner_index)
        score_key, inner_key, other_key, shuffle_key = jax.random.split(owner_seed, 4)
        jitter_score = jax.random.randint(score_key, (space_count,), 0, 1000)
        scores = (jitter_score + 600 * hot) * space_count + devices
        scores = jnp.where(devices == owner_index, -1, scores)
        _, chosen = lax.top_k(scores, groups - 1)
        sources = jnp.concatenate([owner_index[None], chosen.astype(jnp.int32)])

        def group_tiles(group_index):
            middle_tiles = jax.random.permutation(jax.random.fold_in(inner_key, group_index), TILES_DEV - 2)[:CAP - 2] + 1
            forced = jnp.array([0, TILES_DEV - 1], jnp.int32)
            own_tiles = jnp.concatenate([forced, middle_tiles.astype(jnp.int32)])
            others = jax.random.permutation(jax.random.fold_in(other_key, group_index), TILES_DEV)[:CAP].astype(jnp.int32)
            return jnp.where(group_index == 0, own_tiles, others)
        group_picks = jax.vmap(group_tiles)(jnp.arange(groups, dtype=jnp.int32))
        tile_ids = (sources[:, None] * TILES_DEV + group_picks).reshape(-1)
        shuffle = jax.random.permutation(shuffle_key, LIST)
        return tile_ids[shuffle].astype(jnp.int32)
    return jax.vmap(one_owner)(devices)


def steps_of(own_key, extent, cuts, low, top_value):
    level, own = 1.0, jax.random.fold_in(own_key, 6)
    for dim, shards_of in cuts:
        steps = jnp.exp(jax.random.uniform(jax.random.fold_in(own, dim), (shards_of,), jnp.float32, low / len(cuts), top_value / len(cuts)))
        level = level * jnp.repeat(steps, extent[dim] // shards_of).reshape([-1 if axis == dim else 1 for axis in range(len(extent))])
    return level


def bell_draw(key, shape, spread, most, pieces=(), held_as=jnp.bfloat16):
    entries = spread * jax.random.normal(key, shape, jnp.float32)
    if pieces:
        entries = entries * steps_of(key, shape, pieces, -0.22, 0.18)
    return jnp.clip(entries, -most, most).astype(held_as)


def setup_inputs(seed: int = 0) -> dict:
    key_list = jax.random.split(jax.random.key(seed), 5)
    return {
        "basis": draw_basis(jax.random.fold_in(key_list[4], 71), 0),
        "jacobian": bell_draw(key_list[1], (3, F, F, CELLS), (3 * F) ** -0.5, 1.5, ((3, 32),)),
        "sample_list": draw_sample_list(jax.random.fold_in(key_list[4], 71), 0),
        "sample_weight": jnp.clip(jnp.exp(math.log(2.0) - 2.0794415 * jax.random.uniform(key_list[3], (N_SPACE, LIST), jnp.float32) ** steps_of(key_list[3], (N_SPACE, LIST), ((0, 32),), -0.2, 0.2)), 0.25, 2.0),
    }


def forward_apply(neighbor_link, field):
    values = field.astype(jnp.float32)
    edge_zeros = jnp.zeros((values.shape[0], 1), jnp.float32)
    western_cells = jnp.concatenate([edge_zeros, values[:, :-1]], axis=1)
    eastern_cells = jnp.concatenate([values[:, 1:], edge_zeros], axis=1)
    result = jnp.einsum('fgc,gc->fc', neighbor_link[0], values)
    result = result + jnp.einsum('fgc,gc->fc', neighbor_link[1], western_cells)
    return result + jnp.einsum('fgc,gc->fc', neighbor_link[2], eastern_cells)

def adjoint_apply(neighbor_link, quadrature_weight):
    edge_zeros = jnp.zeros((quadrature_weight.shape[0], 1), jnp.float32)
    center_stencil = jnp.einsum('pam,pm->am', neighbor_link[0], quadrature_weight)
    below_stencil = jnp.einsum('pam,pm->am', neighbor_link[1], quadrature_weight)
    above_stencil = jnp.einsum('pam,pm->am', neighbor_link[2], quadrature_weight)
    result = center_stencil + jnp.concatenate([below_stencil[:, 1:], edge_zeros], axis=1)
    return result + jnp.concatenate([edge_zeros, above_stencil[:, :-1]], axis=1)

def reference(basis, jacobian, sample_list, sample_weight):
    neighbor_link = jacobian.astype(jnp.float32)
    operator_result = lax.map(lambda field: forward_apply(neighbor_link, field).astype(jnp.bfloat16), basis)
    owners = sample_list.shape[0]
    tile_view = operator_result.reshape(PANEL, F, TILES, TILE)
    tile_ids = sample_list.reshape(-1).astype(jnp.int32)
    picked = jnp.take(tile_view, tile_ids, axis=2).reshape(PANEL, F, owners, LIST, TILE)
    sample_rows = jnp.einsum('pfolc,ol->opfc', picked.astype(jnp.float32), sample_weight)
    mean_square = lax.optimization_barrier(jnp.sum(sample_rows * sample_rows, axis=(1, 2))) / (PANEL * F)
    normalized = sample_rows * lax.rsqrt(mean_square + 1e-05)[:, None, None, :]
    scaled = (sample_weight[:, :, None, None, None] * normalized[:, None]).astype(jnp.bfloat16)
    flat_rows = scaled.reshape(owners * LIST, PANEL, F, TILE)

    def one_mode(mode_index):
        contribution = jax.ops.segment_sum(flat_rows[:, mode_index].astype(jnp.float32), tile_ids, num_segments=TILES)
        returned = contribution.transpose(1, 0, 2).reshape(F, CELLS)
        return basis[mode_index].astype(jnp.float32) + adjoint_apply(neighbor_link, returned)
    return lax.map(one_mode, jnp.arange(PANEL))
```

```python
import functools

import jax
import jax.numpy as jnp
from jax import lax
from jax.experimental import pallas as pl
from jax.experimental.pallas import tpu as pltpu
from jax.sharding import PartitionSpec as P

F = 5
PANEL = 32
TILE = 128
HALO_NEXT = 16
HALO_PREV = 23
ROWS = 24


def shifted(values, lane_shift):
    lane = lax.broadcasted_iota(jnp.int32, values.shape, 1)
    rolled = pltpu.roll(values, lane_shift % TILE, 1)
    carried = pltpu.roll(rolled, lane_shift % ROWS, 0)
    edge = 0 if lane_shift > 0 else TILE - 1
    return jnp.where(lane == edge, carried, rolled)


def split(values):
    high = values.astype(jnp.bfloat16)
    low = (values - high.astype(jnp.float32)).astype(jnp.bfloat16)
    return high, low


def kernel(
    spaces, modes, here,
    list_ref, weight_ref, basis_ref, jac_ref, out_ref,
    want_send, want, jac_rows, jac, basis_rows, basis, part_send, part, square, norm,
    send_sem, recv_sem,
):
    me = lax.axis_index("space")
    my_mode = lax.axis_index("mode")
    tiles = 16
    q_count = here * F

    def slot(j, q=None):
        return pl.ds(j * q_count, q_count) if q is None else pl.ds(j * q_count + q, 1)

    others = pl.ds(0, (spaces - 1) * q_count)

    def space_at(j):
        return lax.rem(me + 1 + j, spaces)

    def mode_at(j):
        return lax.rem(my_mode + 1 + j, modes)

    barrier = pltpu.get_barrier_semaphore()
    for j in range(spaces - 1):
        pl.semaphore_signal(barrier, inc=1, device_id={"space": space_at(j)})
    for j in range(modes - 1):
        pl.semaphore_signal(barrier, inc=1, device_id={"mode": mode_at(j)})

    row = lax.broadcasted_iota(jnp.int32, (spaces, TILE), 0)
    lane = lax.broadcasted_iota(jnp.int32, (spaces, TILE), 1)
    device = lax.rem(row + (me + 1), spaces)
    offset = jnp.where(lane < tiles + 1, lane, jnp.where(lane == HALO_PREV, -1, -(tiles * spaces + 1)))
    tile_id = device * tiles + offset
    wanted = jnp.zeros((spaces, TILE), jnp.float32)
    for entry in range(list_ref.shape[1]):
        wanted = wanted + jnp.where(tile_id == list_ref[0, entry], weight_ref[0, entry], 0.0)
    want_send[...] = wanted
    want[spaces - 1 :, :] = wanted[spaces - 1 :, :]

    for g in range(F):
        loaded = basis_ref[g].astype(jnp.float32)
        for k in range(tiles):
            basis_rows[g, 8 * k : 8 * k + here, :] = loaded[:, TILE * k : TILE * (k + 1)]
    for p in range(here):
        for g in range(F):
            basis[p * F + g, 0:tiles, :] = basis_rows[g, pl.ds(p, tiles, stride=8), :]

    pl.semaphore_wait(barrier, spaces - 1 + modes - 1)

    def send(src, dst, stage, **where):
        copy = pltpu.make_async_remote_copy(
            src_ref=src, dst_ref=dst, send_sem=send_sem.at[stage], recv_sem=recv_sem.at[stage],
            device_id=where,
        )
        copy.start()

    def arrived(ref, stage):
        pltpu.make_async_copy(ref, ref, recv_sem.at[stage]).wait()

    def left(ref, stage):
        pltpu.make_async_copy(ref, ref, send_sem.at[stage]).wait()

    following = space_at(0)
    previous = space_at(spaces - 2)
    send(basis.at[:, 15, :], basis.at[:, HALO_PREV, :], 0, space=following)
    send(basis.at[:, 0, :], basis.at[:, HALO_NEXT, :], 1, space=previous)
    for j in range(spaces - 1):
        send(want_send.at[pl.ds(j, 1)], want.at[pl.ds(spaces - 2 - j, 1)], 2, space=space_at(j))

    def spread(fg, carry):
        loaded = jac_ref[fg].astype(jnp.float32)
        for k in range(tiles):
            jac_rows[fg, 8 * k : 8 * k + 3, :] = loaded[:, TILE * k : TILE * (k + 1)]
        for w in range(3):
            jac[w * F * F + fg, 0:tiles, :] = jac_rows[fg, pl.ds(w, tiles, stride=8), :]
        return carry

    lax.fori_loop(0, F * F, spread, 0)

    arrived(basis.at[:, HALO_PREV, :], 0)
    arrived(basis.at[:, HALO_NEXT, :], 1)
    first = jnp.where(me == 0, 0.0, 1.0)
    last = jnp.where(me == spaces - 1, 0.0, 1.0)
    edge_row = lax.broadcasted_iota(jnp.int32, (ROWS, TILE), 0)
    keep = jnp.where(edge_row == HALO_PREV, first, jnp.where(edge_row == HALO_NEXT, last, 1.0))
    applied = []
    for p in range(here):
        total = [None] * F
        for g in range(F):
            centre = jnp.where(keep > 0, basis[p * F + g], 0.0)
            moved = (centre, shifted(centre, 1), shifted(centre, -1))
            for f in range(F):
                for w in range(3):
                    term = jac[w * F * F + f * F + g, 0:tiles, :] * moved[w][0:tiles]
                    total[f] = term if total[f] is None else total[f] + term
        applied += [t.astype(jnp.bfloat16) for t in total]
    field = jnp.concatenate(applied, axis=1)

    arrived(want.at[pl.ds(0, spaces - 1)], 2)
    weights = want[...]
    high, low = split(weights)
    partial = jnp.dot(
        jnp.concatenate([high[:, :tiles], low[:, :tiles]], axis=1),
        jnp.concatenate([field, field], axis=0),
        preferred_element_type=jnp.float32,
    )
    for q in range(q_count):
        part_send[pl.ds(q, spaces, stride=q_count), :] = partial[:, q * TILE : (q + 1) * TILE]
    for q in range(q_count):
        part[slot(spaces - 1, q), :] = partial[spaces - 1 :, q * TILE : (q + 1) * TILE]
    for j in range(spaces - 1):
        send(part_send.at[slot(j)], part.at[slot(spaces - 2 - j)], 3, space=space_at(j))
    send(jac.at[pl.ds(F * F, F * F), 0, :], jac.at[pl.ds(F * F, F * F), HALO_NEXT, :], 4, space=previous)
    send(jac.at[pl.ds(2 * F * F, F * F), 15, :], jac.at[pl.ds(2 * F * F, F * F), HALO_PREV, :], 5, space=following)

    turned = jnp.transpose(weights)[0:ROWS]
    turned_high, turned_low = split(turned)
    turned_all = jnp.concatenate([turned_high, turned_low, turned_high], axis=1)

    arrived(part.at[others], 3)
    rows = [
        jnp.sum(part[pl.ds(q, spaces, stride=q_count), :], axis=0, keepdims=True) for q in range(q_count)
    ]
    mine = sum(row * row for row in rows[1:]) + rows[0] * rows[0]
    square[modes - 1 :, :] = mine
    for j in range(modes - 1):
        send(square.at[pl.ds(modes - 1, 1)], square.at[pl.ds(modes - 2 - j, 1)], 6, mode=mode_at(j))
    arrived(square.at[pl.ds(0, modes - 1)], 6)
    mean = jnp.sum(square[...], axis=0, keepdims=True) / (PANEL * F)
    factor = lax.rsqrt(mean + 1e-5)
    for q in range(q_count):
        norm[slot(spaces - 1, q), :] = rows[q] * factor
    for j in range(spaces - 1):
        send(norm.at[slot(spaces - 1)], norm.at[slot(spaces - 2 - j)], 7, space=space_at(j))

    arrived(jac.at[pl.ds(F * F, F * F), HALO_NEXT, :], 4)
    arrived(jac.at[pl.ds(2 * F * F, F * F), HALO_PREV, :], 5)
    arrived(norm.at[others], 7)
    norm_high, norm_low = split(
        jnp.concatenate([norm[pl.ds(q, spaces, stride=q_count), :] for q in range(q_count)], axis=1)
    )
    returned = jnp.dot(
        turned_all,
        jnp.concatenate([norm_high, norm_high, norm_low], axis=0),
        preferred_element_type=jnp.float32,
    )
    for p in range(here):
        for f in range(F):
            parts = []
            for w in range(3):
                total = None
                for g in range(F):
                    q = p * F + g
                    term = jac[w * F * F + g * F + f] * returned[:, q * TILE : (q + 1) * TILE]
                    total = term if total is None else total + term
                parts.append(total)
            update = basis[p * F + f, 0:tiles, :] + parts[0][0:tiles]
            update = update + shifted(parts[1], -1)[0:tiles] + shifted(parts[2], 1)[0:tiles]
            out_ref[f, pl.ds(p, tiles, stride=here), :] = update

    left(basis.at[:, 15, :], 0)
    left(basis.at[:, 0, :], 1)
    left(want_send.at[pl.ds(0, spaces - 1)], 2)
    left(part_send.at[others], 3)
    left(jac.at[pl.ds(F * F, F * F), 0, :], 4)
    left(jac.at[pl.ds(2 * F * F, F * F), 15, :], 5)
    left(square.at[pl.ds(0, modes - 1)], 6)
    left(norm.at[others], 7)


def shards(spaces, modes, basis, jacobian, sample_list, sample_weight):
    here, fields, cells = basis.shape
    tiles = cells // TILE
    vmem = pl.BlockSpec(memory_space=pltpu.VMEM)
    smem = pl.BlockSpec(memory_space=pltpu.SMEM)
    update = pl.pallas_call(
        functools.partial(kernel, spaces, modes, here),
        out_shape=jax.ShapeDtypeStruct((fields, tiles * here, TILE), jnp.float32),
        in_specs=[smem, smem, vmem, vmem],
        out_specs=vmem,
        scratch_shapes=[
            pltpu.VMEM((spaces, TILE), jnp.float32),
            pltpu.VMEM((spaces, TILE), jnp.float32),
            pltpu.VMEM((fields * fields, 8 * tiles, TILE), jnp.float32),
            pltpu.VMEM((3 * fields * fields, ROWS, TILE), jnp.float32),
            pltpu.VMEM((fields, 8 * tiles, TILE), jnp.float32),
            pltpu.VMEM((here * fields, ROWS, TILE), jnp.float32),
            pltpu.VMEM((spaces * here * fields, TILE), jnp.float32),
            pltpu.VMEM((spaces * here * fields, TILE), jnp.float32),
            pltpu.VMEM((modes, TILE), jnp.float32),
            pltpu.VMEM((spaces * here * fields, TILE), jnp.float32),
            pltpu.SemaphoreType.DMA((8,)),
            pltpu.SemaphoreType.DMA((8,)),
        ],
        compiler_params=pltpu.CompilerParams(
            collective_id=0, has_side_effects=True, vmem_limit_bytes=24 * 2**20
        ),
    )(
        sample_list,
        sample_weight,
        basis.transpose(1, 0, 2),
        jacobian.transpose(1, 2, 0, 3).reshape(fields * fields, 3, cells),
    )
    update = update.reshape(fields, tiles, here, TILE).transpose(2, 0, 1, 3)
    return update.reshape(here, fields, cells)


def solution(mesh):
    placed = (
        P("mode", None, "space"),
        P(None, None, None, "space"),
        P("space", None),
        P("space", None),
    )
    return jax.shard_map(
        functools.partial(shards, mesh.shape["space"], mesh.shape["mode"]),
        mesh=mesh, in_specs=placed, out_specs=P("mode", None, "space"), check_vma=False,
    )
```
